256 devices in a mesh: wide: 32 (over z, y), narrow: 8 (over x, core).
Axes of the slice: x: 4, y: 4, z: 8, core: 2. Of those that a mesh axis runs over, the one named last changes fastest.
Arguments:
- user_factors: float32 [262144, 512], P(('wide', 'narrow')), may hold values from -1.25 to 1.25
- item_factors: float32 [256, 2, 512, 512], P(('wide', 'narrow')), may hold values from -1.25 to 1.25
- tile_rows: int32 [256, 5, 2, 10], P(('wide', 'narrow')), may hold values from 0 to 7
- tile_cols: int32 [256, 5, 2, 10], P(('wide', 'narrow')), may hold values from 0 to 3
- tile_count: int32 [256, 5, 2], P(('wide', 'narrow')), may hold values from 2 to 10, as said below
- ratings: bfloat16 [256, 5, 2, 10, 128, 128], P(('wide', 'narrow')), may hold values from -6 to 6
Outputs:
- user_result: float32 [262144, 512], P(('wide', 'narrow'))
- item_result: float32 [256, 2, 512, 512], P(('wide', 'narrow'))
The draws below stay inside these ranges and needn't reach their ends.
Inputs may be any that keep to these rules, and one draw needn't show every extreme that they name: At each visit some stratum has 10 tiles in every slot; entries of tile_rows, tile_cols and ratings at minibatch positions tile_count and beyond are not used.
All inputs are finite; a program needn't handle non-finite values.
Results may differ from the reference program's by a relative error of at most 0.0003.
Values sent between devices are 32-bit elements; how exact they have to be, the bound alone decides.
A program may use at most 64 MiB of HBM per device.

```python
import jax
import jax.numpy as jnp
from jax import lax

RANK = 512
TILE = 128
ITEMS_PER_BLOCK = 512
USER_DEV = 1024
SLOTS = 2
SWEEP_TOTAL = 5
TILES_MOST = 10
CUSTOMER_LAYERS = 256
USERS = 262144
N_WIDE = 32
N_NARROW = 8


def draw_tile_count(key, part):
    shuffle_wave_seed, selected_seed, smaller_submatrix_seed = jax.random.split(key, 3)
    larger_submatrix = jax.random.randint(shuffle_wave_seed, (CUSTOMER_LAYERS, SWEEP_TOTAL, 1), 0, 8) == 0
    chosen = jax.random.randint(selected_seed, (1, SWEEP_TOTAL, 1), 0, CUSTOMER_LAYERS)
    position = jnp.arange(CUSTOMER_LAYERS).reshape(CUSTOMER_LAYERS, 1, 1)
    larger_submatrix = jnp.logical_or(larger_submatrix, position == chosen)
    lighter = jax.random.randint(smaller_submatrix_seed, (CUSTOMER_LAYERS, SWEEP_TOTAL, SLOTS), 2, TILES_MOST // 2 + 1)
    return jnp.where(larger_submatrix, TILES_MOST, lighter).astype(jnp.int32)


def with_ends(drawn, rng, low, high):
    dims = drawn.shape
    place = [jax.random.randint(jax.random.fold_in(rng, axis), (), 0, dims[axis]) for axis in range(len(dims))]
    drawn = drawn.at[tuple(place)].set(low)
    longest = dims.index(max(dims))
    place[longest] = (place[longest] + 1) % dims[longest]
    return drawn.at[tuple(place)].set(high)


def level_of(key, dims, shards, least, high):
    def one(axis_at, blocks):
        steps = jax.random.uniform(jax.random.fold_in(jax.random.fold_in(key, 6), axis_at), (blocks,), jnp.float32, least / len(shards), high / len(shards))
        return jnp.repeat(jnp.exp(steps), dims[axis_at] // blocks).reshape((-1,) + (1,) * (len(dims) - axis_at - 1))

    gain = one(*shards[0])
    for cut in shards[1:]:
        gain = gain * one(*cut)
    return gain


def scatter_about(own_key, shape, width, bound, shards=(), kind=jnp.bfloat16):
    result = width * jax.random.normal(own_key, shape, jnp.float32)
    if shards:
        result = result * level_of(own_key, shape, shards, -0.22, 0.18)
    return jnp.clip(result, -bound, bound).astype(kind)


def setup_inputs(seed: int = 0) -> dict:
    seeds = jax.random.split(jax.random.key(seed), 7)
    return {
        "user_factors": scatter_about(seeds[0], (USERS, RANK), (RANK ** -0.25), 1.25, ((0, 256),), jnp.float32),
        "item_factors": scatter_about(seeds[1], (CUSTOMER_LAYERS, SLOTS, ITEMS_PER_BLOCK, RANK), (RANK ** -0.25), 1.25, ((0, 256),), jnp.float32),
        "tile_rows": with_ends(jax.random.randint(seeds[2], (CUSTOMER_LAYERS, SWEEP_TOTAL, SLOTS, TILES_MOST), 0, USER_DEV // TILE), jax.random.fold_in(seeds[2], 1), 0, (USER_DEV // TILE) - 1).astype(jnp.int32),
        "tile_cols": with_ends(jax.random.randint(seeds[3], (CUSTOMER_LAYERS, SWEEP_TOTAL, SLOTS, TILES_MOST), 0, ITEMS_PER_BLOCK // TILE), jax.random.fold_in(seeds[3], 1), 0, (ITEMS_PER_BLOCK // TILE) - 1).astype(jnp.int32),
        "tile_count": draw_tile_count(jax.random.fold_in(seeds[6], 71), 0),
        "ratings": scatter_about(seeds[5], (CUSTOMER_LAYERS, SWEEP_TOTAL, SLOTS, TILES_MOST, TILE, TILE), 1.0, 6.0, ((0, 256),)),
    }


learn_rate = 0.0035
decay_weight = 0.05


def tile_update(user_block, item_block, rating_tile, row_tile, col_tile):
    tile_size = rating_tile.shape[-1]
    users_part = lax.dynamic_slice_in_dim(user_block, row_tile * tile_size, tile_size, 0)
    items_part = lax.dynamic_slice_in_dim(item_block, col_tile * tile_size, tile_size, 0)
    predicted = lax.dot_general(users_part, items_part, (((1,), (1,)), ((), ())), precision=lax.Precision.HIGHEST, preferred_element_type=jnp.float32)
    errors = predicted - rating_tile.astype(jnp.float32)
    user_grad = jnp.dot(errors, items_part, precision=lax.Precision.HIGHEST, preferred_element_type=jnp.float32) + decay_weight * users_part
    item_gradient = lax.dot_general(errors, users_part, (((0,), (0,)), ((), ())), precision=lax.Precision.HIGHEST, preferred_element_type=jnp.float32) + decay_weight * items_part
    new_users = users_part - learn_rate * user_grad
    new_items = items_part - learn_rate * item_gradient
    user_block = lax.dynamic_update_slice_in_dim(user_block, new_users, row_tile * tile_size, 0)
    item_block = lax.dynamic_update_slice_in_dim(item_block, new_items, col_tile * tile_size, 0)
    return user_block, item_block


def sweep_slot(user_block, item_block, ratings_slot, rows_slot, cols_slot, tile_total):
    def one_tile(position, carried):
        user_now, item_now = carried
        return tile_update(user_now, item_now, ratings_slot[position], rows_slot[position], cols_slot[position])

    return lax.fori_loop(0, tile_total, one_tile, (user_block, item_block))


def reference(user_factors, item_factors, tile_rows, tile_cols, tile_count, ratings):
    user_blocks = user_factors.reshape(CUSTOMER_LAYERS, USER_DEV, RANK)
    held_blocks = item_factors
    for visit_index in range(SWEEP_TOTAL):
        if visit_index > 0:
            layout_grid = held_blocks.reshape(N_WIDE, N_NARROW, SLOTS, ITEMS_PER_BLOCK, RANK)
            layout_grid = jnp.roll(layout_grid, 1, axis=0)
            if visit_index == SWEEP_TOTAL - 1:
                layout_grid = jnp.roll(layout_grid, 1, axis=1)
            held_blocks = layout_grid.reshape(CUSTOMER_LAYERS, SLOTS, ITEMS_PER_BLOCK, RANK)
        new_slots = []
        for holder_position in range(SLOTS):
            user_blocks, holder_product_factors = jax.vmap(sweep_slot)(
                user_blocks,
                held_blocks[:, holder_position],
                ratings[:, visit_index, holder_position],
                tile_rows[:, visit_index, holder_position],
                tile_cols[:, visit_index, holder_position],
                tile_count[:, visit_index, holder_position],
            )
            new_slots.append(holder_product_factors)
        held_blocks = jnp.stack(new_slots, axis=1)
    return (user_blocks.reshape(USERS, RANK), held_blocks)
```

```python
import functools

import jax
import jax.numpy as jnp
from jax import lax
from jax.experimental import pallas as pl
from jax.experimental.pallas import tpu as pltpu
from jax.sharding import PartitionSpec as P

learn_rate = 0.0035
decay_weight = 0.05

RING = 4
TILE = 128
RELAY_ROWS = 112
MESH = pl.DeviceIdType.MESH


def split(x):
    high = x.astype(jnp.bfloat16)
    return high, (x - high.astype(jnp.float32)).astype(jnp.bfloat16)


def tile_update(users, items, rating):
    uh, ul = split(users)
    ih, il = split(items)
    s = lax.dot_general(
        jnp.concatenate([uh, ul], 0),
        jnp.concatenate([ih, il], 0),
        (((1,), (1,)), ((), ())),
        preferred_element_type=jnp.float32,
    )
    t = TILE
    errors = (s[:t, :t] + (s[:t, t:] + s[t:, :t])) - rating.astype(jnp.float32)
    eh, el = split(errors)
    user_grad = jnp.dot(
        jnp.concatenate([eh, el, eh], 1),
        jnp.concatenate([ih, ih, il], 0),
        preferred_element_type=jnp.float32,
    )
    th, tl = split(errors.T)
    item_grad = jnp.dot(
        jnp.concatenate([th, tl, th], 1),
        jnp.concatenate([uh, uh, ul], 0),
        preferred_element_type=jnp.float32,
    )
    new_users = users - learn_rate * (user_grad + decay_weight * users)
    new_items = items - learn_rate * (item_grad + decay_weight * items)
    return new_users, new_items


def pick(values, index):
    out = values[0]
    for i in range(1, len(values)):
        out = jnp.where(index == i, values[i], out)
    return out


def kernel(
    n_wide,
    n_narrow,
    visits,
    slots,
    most,
    users_ref,
    items_ref,
    ratings_ref,
    rows_ref,
    cols_ref,
    count_ref,
    users_out,
    items_out,
    users,
    work,
    held,
    relay_one,
    relay_two,
    ratings,
    load_sem,
    rating_sem,
    send_sem,
    recv_sem,
):
    steps = visits * slots
    moves = steps - slots
    user_tiles = users_ref.shape[0]
    block_rows = items_ref.shape[2]
    item_tiles = block_rows // TILE
    straight = block_rows - RELAY_ROWS

    w = lax.axis_index("wide")
    n = lax.axis_index("narrow")
    y = lax.rem(w, RING)
    base = w - y
    after = lax.rem(w + 1, n_wide)
    before = lax.rem(w + n_wide - 1, n_wide)
    down = base + lax.rem(y + RING - 1, RING)
    up = base + lax.rem(y + 1, RING)
    third_to = lax.rem(down + jnp.where(y == RING - 3, RING, 0), n_wide)
    third_from = lax.rem(up + n_wide - jnp.where(y == 0, RING, 0), n_wide)
    n_after = lax.rem(n + 1, n_narrow)
    n_before = lax.rem(n + n_narrow - 1, n_narrow)

    loads = [
        pltpu.make_async_copy(items_ref.at[0, 0], held.at[0], load_sem.at[0]),
        pltpu.make_async_copy(users_ref, users.at[pl.ds(0, user_tiles)], load_sem.at[2]),
        pltpu.make_async_copy(items_ref.at[0, 1], held.at[1], load_sem.at[1]),
    ]

    def rating_copy(t):
        return pltpu.make_async_copy(
            ratings_ref.at[0, t // slots, lax.rem(t, slots)], ratings.at[t], rating_sem.at[t]
        )

    loads[0].start()
    loads[1].start()
    rating_copy(0).start()
    loads[2].start()
    for t in range(1, steps):
        rating_copy(t).start()

    barrier = pltpu.get_barrier_semaphore()
    partners = [
        (after, n),
        (before, n),
        (down, n),
        (up, n),
        (third_to, n),
        (third_from, n),
        (after, n_after),
        (before, n_before),
        (third_to, n_after),
        (third_from, n_before),
    ]
    for partner in partners:
        pl.semaphore_signal(barrier, inc=1, device_id=partner, device_id_type=MESH)
    pl.semaphore_wait(barrier, len(partners))

    def remote(kind, t, src, dst, device):
        return pltpu.make_async_remote_copy(
            src_ref=src,
            dst_ref=dst,
            send_sem=send_sem.at[kind, t],
            recv_sem=recv_sem.at[kind, t],
            device_id=device,
            device_id_type=MESH,
        )

    def ending_n(t):
        return jnp.where(t >= moves - slots, n_after, n)

    def direct(t):
        rows = pl.ds(0, straight)
        return remote(0, t, held.at[t, rows], held.at[t + slots, rows], (after, ending_n(t)))

    def hop_one(t):
        return remote(1, t, held.at[t, pl.ds(straight, RELAY_ROWS)], relay_one.at[t], (down, n))

    def hop_two(t):
        return remote(2, t, relay_one.at[t], relay_two.at[t], (down, n))

    def hop_three(t):
        rows = pl.ds(straight, RELAY_ROWS)
        return remote(3, t, relay_two.at[t], held.at[t + slots, rows], (third_to, ending_n(t)))

    loads[0].wait()
    loads[1].wait()

    def step(t, carry):
        visit, slot = t // slots, lax.rem(t, slots)
        count = count_ref[0, visit, slot]

        @pl.when(t == 1)
        def _():
            loads[2].wait()

        rating_copy(t).wait()

        @pl.when(t >= slots)
        def _():
            direct(t - slots).wait_recv()
            hop_three(t - slots).wait_recv()

        for i in range(item_tiles):
            work[i] = held[t, i * TILE : (i + 1) * TILE, :]

        def one(k, state):
            user_at, item_at = state
            live = k < count
            a = jnp.where(live, rows_ref[0, visit, slot, k], 0)
            c = jnp.where(live, cols_ref[0, visit, slot, k], 0)
            ua = pick(user_at, a)
            ia = pick(item_at, c)
            new_users, new_items = tile_update(
                users[ua],
                work[ia],
                ratings[t, k],
            )
            users[user_tiles + k] = new_users
            work[item_tiles + k] = new_items
            user_at = tuple(
                jnp.where(live & (a == i), user_tiles + k, v) for i, v in enumerate(user_at)
            )
            item_at = tuple(
                jnp.where(live & (c == i), item_tiles + k, v) for i, v in enumerate(item_at)
            )
            return user_at, item_at

        state = (
            tuple(jnp.int32(i) for i in range(user_tiles)),
            tuple(jnp.int32(i) for i in range(item_tiles)),
        )
        state = lax.fori_loop(0, most // 2, one, state)

        @pl.when((t >= 1) & (t <= moves))
        def _():
            hop_one(t - 1).wait_recv()
            hop_two(t - 1).start()

        user_at, item_at = lax.fori_loop(most // 2, most, one, state)

        for i in range(item_tiles):
            held[t, i * TILE : (i + 1) * TILE, :] = work[item_at[i]]

        @pl.when(t < moves)
        def _():
            hop_one(t).start()
            direct(t).start()

        for i in range(user_tiles):
            users[i] = users[user_at[i]]

        @pl.when((t >= 1) & (t <= moves))
        def _():
            hop_two(t - 1).wait_recv()
            hop_three(t - 1).start()

        return carry

    lax.fori_loop(0, steps, step, 0)

    stores = [
        pltpu.make_async_copy(users.at[pl.ds(0, user_tiles)], users_out, load_sem.at[2])
    ]
    for s in range(slots):
        stores.append(
            pltpu.make_async_copy(held.at[moves + s], items_out.at[0, s], load_sem.at[s])
        )
    for copy in stores:
        copy.start()

    def drain(t, carry):
        for make in (direct, hop_one, hop_two, hop_three):
            make(t).wait_send()
        return carry

    lax.fori_loop(0, moves, drain, 0)
    for copy in stores:
        copy.wait()


def body(n_wide, n_narrow, user_factors, item_factors, tile_rows, tile_cols, tile_count, ratings):
    visits, slots, most = tile_rows.shape[1:]
    steps = visits * slots
    moves = steps - slots
    rank = user_factors.shape[1]
    user_tiles = user_factors.shape[0] // TILE
    user_blocks = user_factors.reshape(user_tiles, TILE, rank)
    block_rows = item_factors.shape[2]
    anywhere = pl.BlockSpec(memory_space=pl.ANY)
    smem = pl.BlockSpec(memory_space=pltpu.SMEM)
    f32 = jnp.float32
    users_new, items_new = pl.pallas_call(
        functools.partial(kernel, n_wide, n_narrow, visits, slots, most),
        out_shape=(
            jax.ShapeDtypeStruct(user_blocks.shape, f32),
            jax.ShapeDtypeStruct(item_factors.shape, f32),
        ),
        in_specs=[anywhere, anywhere, anywhere, smem, smem, smem],
        out_specs=(anywhere, anywhere),
        scratch_shapes=[
            pltpu.VMEM((user_tiles + most, TILE, rank), f32),
            pltpu.VMEM((block_rows // TILE + most, TILE, rank), f32),
            pltpu.VMEM((steps, block_rows, rank), f32),
            pltpu.VMEM((moves, RELAY_ROWS, rank), f32),
            pltpu.VMEM((moves, RELAY_ROWS, rank), f32),
            pltpu.VMEM((steps, most, TILE, TILE), ratings.dtype),
            pltpu.SemaphoreType.DMA((3,)),
            pltpu.SemaphoreType.DMA((steps,)),
            pltpu.SemaphoreType.DMA((4, moves)),
            pltpu.SemaphoreType.DMA((4, moves)),
        ],
        compiler_params=pltpu.CompilerParams(
            collective_id=0, has_side_effects=True, vmem_limit_bytes=40 << 20
        ),
        name="sgd_sweep",
    )(user_blocks, item_factors, ratings, tile_rows, tile_cols, tile_count)
    return users_new.reshape(user_factors.shape), items_new


def solution(mesh):
    both = ("wide", "narrow")
    in_specs = (
        P(both, None),
        P(both, None, None, None),
        P(both, None, None, None),
        P(both, None, None, None),
        P(both, None, None),
        P(both, None, None, None, None, None),
    )
    out_specs = (P(both, None), P(both, None, None, None))
    run = functools.partial(body, mesh.shape["wide"], mesh.shape["narrow"])
    return jax.shard_map(run, mesh=mesh, in_specs=in_specs, out_specs=out_specs, check_vma=False)
```

```python
import functools

import jax
import jax.numpy as jnp
from jax import lax
from jax.experimental import pallas as pl
from jax.experimental.pallas import tpu as pltpu
from jax.sharding import PartitionSpec as P

learn_rate = 0.0035
decay_weight = 0.05

RING = 4
TILE = 128
RELAY_ROWS = 128
CHUNKS = 2
CHUNK_ROWS = RELAY_ROWS // CHUNKS
FORWARDS = ((0, 2, 0), (2, 2, 1), (4, 3, 0), (8, 3, 1))
MESH = pl.DeviceIdType.MESH


def split(x):
    high = x.astype(jnp.bfloat16)
    return high, (x - high.astype(jnp.float32)).astype(jnp.bfloat16)


def step_of(products, rating):
    t = TILE
    errors = (products[:t, :t] + (products[:t, t:] + products[t:, :t])) - rating
    return errors * -learn_rate


def tile_update(users, items, rating):
    uh, ul = split(users)
    ih, il = split(items)
    rating = rating.astype(jnp.float32)
    u_both, i_both = jnp.concatenate([uh, ul], 0), jnp.concatenate([ih, il], 0)
    rows_by_rows = (((1,), (1,)), ((), ()))
    f32 = jnp.float32
    s = lax.dot_general(u_both, i_both, rows_by_rows, preferred_element_type=f32)
    s_turned = lax.dot_general(i_both, u_both, rows_by_rows, preferred_element_type=f32)
    eh, el = split(step_of(s, rating))
    th, tl = split(step_of(s_turned, rating.T))
    user_step = jnp.dot(
        jnp.concatenate([eh, el, eh], 1),
        jnp.concatenate([ih, ih, il], 0),
        preferred_element_type=f32,
    )
    item_step = jnp.dot(
        jnp.concatenate([th, tl, th], 1),
        jnp.concatenate([uh, uh, ul], 0),
        preferred_element_type=f32,
    )
    keep = 1.0 - learn_rate * decay_weight
    return users * keep + user_step, items * keep + item_step


def pick(values, index):
    out = values[0]
    for i in range(1, len(values)):
        out = jnp.where(index == i, values[i], out)
    return out


def kernel(
    n_wide,
    n_narrow,
    visits,
    slots,
    most,
    users_ref,
    items_ref,
    ratings_ref,
    rows_ref,
    cols_ref,
    count_ref,
    users_out,
    items_out,
    users,
    work,
    held,
    relay_one,
    relay_two,
    ratings,
    load_sem,
    rating_sem,
    send_sem,
    recv_sem,
):
    steps = visits * slots
    moves = steps - slots
    user_tiles = users_ref.shape[0]
    block_rows = items_ref.shape[2]
    item_tiles = block_rows // TILE
    straight = block_rows - RELAY_ROWS

    w = lax.axis_index("wide")
    n = lax.axis_index("narrow")
    y = lax.rem(w, RING)
    base = w - y
    after = lax.rem(w + 1, n_wide)
    before = lax.rem(w + n_wide - 1, n_wide)
    down = base + lax.rem(y + RING - 1, RING)
    up = base + lax.rem(y + 1, RING)
    third_to = lax.rem(down + jnp.where(y == RING - 3, RING, 0), n_wide)
    third_from = lax.rem(up + n_wide - jnp.where(y == 0, RING, 0), n_wide)
    n_after = lax.rem(n + 1, n_narrow)
    n_before = lax.rem(n + n_narrow - 1, n_narrow)

    loads = [
        pltpu.make_async_copy(items_ref.at[0, 0], held.at[0], load_sem.at[0]),
        pltpu.make_async_copy(users_ref, users.at[pl.ds(0, user_tiles)], load_sem.at[2]),
        pltpu.make_async_copy(items_ref.at[0, 1], held.at[1], load_sem.at[1]),
    ]

    def rating_copy(t):
        return pltpu.make_async_copy(
            ratings_ref.at[0, t // slots, lax.rem(t, slots)], ratings.at[t], rating_sem.at[t]
        )

    loads[0].start()
    loads[1].start()
    rating_copy(0).start()
    barrier = pltpu.get_barrier_semaphore()
    partners = [
        (after, n),
        (before, n),
        (down, n),
        (up, n),
        (third_to, n),
        (third_from, n),
        (after, n_after),
        (before, n_before),
        (third_to, n_after),
        (third_from, n_before),
    ]
    for partner in partners:
        pl.semaphore_signal(barrier, inc=1, device_id=partner, device_id_type=MESH)
    pl.semaphore_wait(barrier, len(partners))

    def remote(kind, t, src, dst, device):
        return pltpu.make_async_remote_copy(
            src_ref=src,
            dst_ref=dst,
            send_sem=send_sem.at[kind, t],
            recv_sem=recv_sem.at[kind, t],
            device_id=device,
            device_id_type=MESH,
        )

    def ending_n(t):
        return jnp.where(t >= moves - slots, n_after, n)

    def direct(t):
        rows = pl.ds(0, straight)
        return remote(0, t, held.at[t, rows], held.at[t + slots, rows], (after, ending_n(t)))

    def hop(number, chunk, t):
        kind = 1 + (number - 1) * CHUNKS + chunk
        rows = pl.ds(straight + chunk * CHUNK_ROWS, CHUNK_ROWS)
        if number == 1:
            src, dst, device = held.at[t, rows], relay_one.at[t, chunk], (down, n)
        elif number == 2:
            src, dst, device = relay_one.at[t, chunk], relay_two.at[t, chunk], (down, n)
        else:
            src, dst = relay_two.at[t, chunk], held.at[t + slots, rows]
            device = (third_to, ending_n(t))
        return remote(kind, t, src, dst, device)

    loads[0].wait()
    loads[1].wait()
    loads[2].start()
    for t in range(1, steps):
        rating_copy(t).start()

    def step(t, carry):
        visit, slot = t // slots, lax.rem(t, slots)
        count = count_ref[0, slot, visit]

        @pl.when(t == 1)
        def _():
            loads[2].wait()

        rating_copy(t).wait()

        @pl.when(t >= slots)
        def _():
            direct(t - slots).wait_recv()
            for chunk in range(CHUNKS):
                hop(3, chunk, t - slots).wait_recv()

        for i in range(item_tiles):
            work[i] = held[t, i * TILE : (i + 1) * TILE, :]

        def one(k, state):
            user_at, item_at = state
            live = k < count
            a = jnp.where(live, rows_ref[0, visit, slot, k], 0)
            c = jnp.where(live, cols_ref[0, visit, slot, k], 0)
            ua = pick(user_at, a)
            ia = pick(item_at, c)
            new_users, new_items = tile_update(
                users[ua],
                work[ia],
                ratings[t, k],
            )
            users[user_tiles + k] = new_users
            work[item_tiles + k] = new_items
            user_at = tuple(
                jnp.where(live & (a == i), user_tiles + k, v) for i, v in enumerate(user_at)
            )
            item_at = tuple(
                jnp.where(live & (c == i), item_tiles + k, v) for i, v in enumerate(item_at)
            )
            return user_at, item_at

        state = (
            tuple(jnp.int32(i) for i in range(user_tiles)),
            tuple(jnp.int32(i) for i in range(item_tiles)),
        )
        done = 0
        for position, number, chunk in FORWARDS:
            if position > done:
                state = lax.fori_loop(done, position, one, state, unroll=2)
                done = position

            @pl.when((t >= 1) & (t <= moves))
            def _():
                hop(number - 1, chunk, t - 1).wait_recv()
                hop(number, chunk, t - 1).start()

        if done < most:
            state = lax.fori_loop(done, most, one, state, unroll=2)
        user_at, item_at = state

        for i in range(item_tiles):
            held[t, i * TILE : (i + 1) * TILE, :] = work[item_at[i]]

        @pl.when(t < moves)
        def _():
            for chunk in range(CHUNKS):
                hop(1, chunk, t).start()
            direct(t).start()

        for i in range(user_tiles):
            users[i] = users[user_at[i]]

        return carry

    lax.fori_loop(0, steps, step, 0)

    stores = [
        pltpu.make_async_copy(users.at[pl.ds(0, user_tiles)], users_out, load_sem.at[2])
    ]
    for s in range(slots):
        stores.append(
            pltpu.make_async_copy(held.at[moves + s], items_out.at[0, s], load_sem.at[s])
        )
    for copy in stores:
        copy.start()

    def drain(t, carry):
        direct(t).wait_send()
        for number in (1, 2, 3):
            for chunk in range(CHUNKS):
                hop(number, chunk, t).wait_send()
        return carry

    lax.fori_loop(0, moves, drain, 0)
    for copy in stores:
        copy.wait()


def body(n_wide, n_narrow, user_factors, item_factors, tile_rows, tile_cols, tile_count, ratings):
    visits, slots, most = tile_rows.shape[1:]
    steps = visits * slots
    moves = steps - slots
    rank = user_factors.shape[1]
    user_tiles = user_factors.shape[0] // TILE
    user_blocks = user_factors.reshape(user_tiles, TILE, rank)
    block_rows = item_factors.shape[2]
    anywhere = pl.BlockSpec(memory_space=pl.ANY)
    hbm = pl.BlockSpec(memory_space=pltpu.HBM)
    smem = pl.BlockSpec(memory_space=pltpu.SMEM)
    f32 = jnp.float32
    users_new, items_new = pl.pallas_call(
        functools.partial(kernel, n_wide, n_narrow, visits, slots, most),
        out_shape=(
            jax.ShapeDtypeStruct(user_blocks.shape, f32),
            jax.ShapeDtypeStruct(item_factors.shape, f32),
        ),
        in_specs=[hbm, hbm, hbm, smem, smem, smem],
        out_specs=(anywhere, anywhere),
        scratch_shapes=[
            pltpu.VMEM((user_tiles + most, TILE, rank), f32),
            pltpu.VMEM((block_rows // TILE + most, TILE, rank), f32),
            pltpu.VMEM((steps, block_rows, rank), f32),
            pltpu.VMEM((moves, CHUNKS, CHUNK_ROWS, rank), f32),
            pltpu.VMEM((moves, CHUNKS, CHUNK_ROWS, rank), f32),
            pltpu.VMEM((steps, most, TILE, TILE), ratings.dtype),
            pltpu.SemaphoreType.DMA((3,)),
            pltpu.SemaphoreType.DMA((steps,)),
            pltpu.SemaphoreType.DMA((1 + 3 * CHUNKS, moves)),
            pltpu.SemaphoreType.DMA((1 + 3 * CHUNKS, moves)),
        ],
        compiler_params=pltpu.CompilerParams(
            collective_id=0, has_side_effects=True, vmem_limit_bytes=56 << 20
        ),
        name="sgd_sweep",
    )(user_blocks, item_factors, ratings, tile_rows, tile_cols, tile_count.swapaxes(1, 2))
    return users_new.reshape(user_factors.shape), items_new


def solution(mesh):
    both = ("wide", "narrow")
    in_specs = (
        P(both, None),
        P(both, None, None, None),
        P(both, None, None, None),
        P(both, None, None, None),
        P(both, None, None),
        P(both, None, None, None, None, None),
    )
    out_specs = (P(both, None), P(both, None, None, None))
    run = functools.partial(body, mesh.shape["wide"], mesh.shape["narrow"])
    return jax.shard_map(run, mesh=mesh, in_specs=in_specs, out_specs=out_specs, check_vma=False)
```

```python
import functools

import jax
import jax.numpy as jnp
from jax import lax
from jax.experimental import pallas as pl
from jax.experimental.pallas import tpu as pltpu
from jax.sharding import PartitionSpec as P

learn_rate = 0.0035
decay_weight = 0.05

RING = 4
TILE = 128
RELAY_ROWS = 128
VMEM_GRANT = 56 << 20
CHUNKS = 2
CHUNK_ROWS = RELAY_ROWS // CHUNKS
FORWARDS = ((0, 2, 0), (2, 2, 1), (4, 3, 0), (8, 3, 1))
MESH = pl.DeviceIdType.MESH


def split(x):
    high = x.astype(jnp.bfloat16)
    return high, (x - high.astype(jnp.float32)).astype(jnp.bfloat16)


def step_of(products, rating):
    t = TILE
    errors = (products[:t, :t] + (products[:t, t:] + products[t:, :t])) - rating
    return errors * -learn_rate


def tile_update(users, items, rating):
    uh, ul = split(users)
    ih, il = split(items)
    rating = rating.astype(jnp.float32)
    u_both, i_both = jnp.concatenate([uh, ul], 0), jnp.concatenate([ih, il], 0)
    rows_by_rows = (((1,), (1,)), ((), ()))
    f32 = jnp.float32
    s = lax.dot_general(u_both, i_both, rows_by_rows, preferred_element_type=f32)
    s_turned = lax.dot_general(i_both, u_both, rows_by_rows, preferred_element_type=f32)
    eh, el = split(step_of(s, rating))
    th, tl = split(step_of(s_turned, rating.T))
    user_step = jnp.dot(
        jnp.concatenate([eh, el, eh], 1),
        jnp.concatenate([ih, ih, il], 0),
        preferred_element_type=f32,
    )
    item_step = jnp.dot(
        jnp.concatenate([th, tl, th], 1),
        jnp.concatenate([uh, uh, ul], 0),
        preferred_element_type=f32,
    )
    keep = 1.0 - learn_rate * decay_weight
    return users * keep + user_step, items * keep + item_step


def pick(values, index):
    out = values[0]
    for i in range(1, len(values)):
        out = jnp.where(index == i, values[i], out)
    return out


def kernel(
    n_wide,
    n_narrow,
    visits,
    slots,
    most,
    users_ref,
    items_ref,
    ratings_ref,
    rows_ref,
    cols_ref,
    count_ref,
    users_out,
    blocks_out,
    users,
    work,
    held,
    relay_one,
    relay_two,
    ratings,
    load_sem,
    rating_sem,
    send_sem,
    recv_sem,
):
    steps = visits * slots
    moves = steps - slots
    user_tiles = users_ref.shape[0]
    block_rows = items_ref.shape[2]
    item_tiles = block_rows // TILE
    straight = block_rows - RELAY_ROWS

    w = lax.axis_index("wide")
    n = lax.axis_index("narrow")
    y = lax.rem(w, RING)
    base = w - y
    after = lax.rem(w + 1, n_wide)
    before = lax.rem(w + n_wide - 1, n_wide)
    down = base + lax.rem(y + RING - 1, RING)
    up = base + lax.rem(y + 1, RING)
    third_to = lax.rem(down + jnp.where(y == RING - 3, RING, 0), n_wide)
    third_from = lax.rem(up + n_wide - jnp.where(y == 0, RING, 0), n_wide)
    n_after = lax.rem(n + 1, n_narrow)
    n_before = lax.rem(n + n_narrow - 1, n_narrow)

    loads = [
        pltpu.make_async_copy(items_ref.at[0, 0], held.at[0], load_sem.at[0]),
        pltpu.make_async_copy(users_ref, users.at[pl.ds(0, user_tiles)], load_sem.at[2]),
        pltpu.make_async_copy(items_ref.at[0, 1], held.at[1], load_sem.at[1]),
    ]

    def rating_copy(t):
        return pltpu.make_async_copy(
            ratings_ref.at[0, t // slots, lax.rem(t, slots)], ratings.at[t], rating_sem.at[t]
        )

    loads[0].start()
    loads[1].start()
    rating_copy(0).start()
    barrier = pltpu.get_barrier_semaphore()
    partners = [
        (after, n),
        (before, n),
        (down, n),
        (up, n),
        (third_to, n),
        (third_from, n),
        (after, n_after),
        (before, n_before),
        (third_to, n_after),
        (third_from, n_before),
    ]
    for partner in partners:
        pl.semaphore_signal(barrier, inc=1, device_id=partner, device_id_type=MESH)
    pl.semaphore_wait(barrier, len(partners))

    def remote(kind, t, src, dst, device):
        return pltpu.make_async_remote_copy(
            src_ref=src,
            dst_ref=dst,
            send_sem=send_sem.at[kind, t],
            recv_sem=recv_sem.at[kind, t],
            device_id=device,
            device_id_type=MESH,
        )

    def ending_n(t):
        return jnp.where(t >= moves - slots, n_after, n)

    def direct(t):
        rows = pl.ds(0, straight)
        return remote(0, t, held.at[t, rows], held.at[t + slots, rows], (after, ending_n(t)))

    def hop(number, chunk, t):
        kind = 1 + (number - 1) * CHUNKS + chunk
        rows = pl.ds(straight + chunk * CHUNK_ROWS, CHUNK_ROWS)
        if number == 1:
            src, dst, device = held.at[t, rows], relay_one.at[t, chunk], (down, n)
        elif number == 2:
            src, dst, device = relay_one.at[t, chunk], relay_two.at[t, chunk], (down, n)
        else:
            src, dst = relay_two.at[t, chunk], held.at[t + slots, rows]
            device = (third_to, ending_n(t))
        return remote(kind, t, src, dst, device)

    loads[0].wait()
    loads[1].wait()
    loads[2].start()
    for t in range(1, moves + 1):
        rating_copy(t).start()

    def step(t, carry):
        visit, slot = t // slots, lax.rem(t, slots)
        count = count_ref[0, slot, visit]

        @pl.when(t == 1)
        def _():
            loads[2].wait()

        rating_copy(t).wait()

        @pl.when(t >= slots)
        def _():
            direct(t - slots).wait_recv()
            for chunk in range(CHUNKS):
                hop(3, chunk, t - slots).wait_recv()

        for i in range(item_tiles):
            work[i] = held[t, i * TILE : (i + 1) * TILE, :]

        def one(k, state):
            user_at, item_at = state
            live = k < count
            a = jnp.where(live, rows_ref[0, visit, slot, k], 0)
            c = jnp.where(live, cols_ref[0, visit, slot, k], 0)
            ua = pick(user_at, a)
            ia = pick(item_at, c)
            new_users, new_items = tile_update(
                users[ua],
                work[ia],
                ratings[t, k],
            )
            users[user_tiles + k] = new_users
            work[item_tiles + k] = new_items
            user_at = tuple(
                jnp.where(live & (a == i), user_tiles + k, v) for i, v in enumerate(user_at)
            )
            item_at = tuple(
                jnp.where(live & (c == i), item_tiles + k, v) for i, v in enumerate(item_at)
            )
            return user_at, item_at

        state = (
            tuple(jnp.int32(i) for i in range(user_tiles)),
            tuple(jnp.int32(i) for i in range(item_tiles)),
        )
        done = 0
        for position, number, chunk in FORWARDS:
            if position > done:
                state = lax.fori_loop(done, position, one, state, unroll=2)
                done = position

            @pl.when((t >= 1) & (t <= moves))
            def _():
                hop(number - 1, chunk, t - 1).wait_recv()
                hop(number, chunk, t - 1).start()

        if done < most:
            state = lax.fori_loop(done, most, one, state, unroll=2)
        user_at, item_at = state

        for i in range(item_tiles):
            held[t, i * TILE : (i + 1) * TILE, :] = work[item_at[i]]

        @pl.when(t < moves)
        def _():
            for chunk in range(CHUNKS):
                hop(1, chunk, t).start()
            direct(t).start()

        for i in range(user_tiles):
            users[i] = users[user_at[i]]

        return carry

    lax.fori_loop(0, moves + 1, step, 0)

    stores = [
        pltpu.make_async_copy(users.at[pl.ds(0, user_tiles)], users_out, load_sem.at[2]),
        pltpu.make_async_copy(held.at[moves], blocks_out.at[0], load_sem.at[0]),
    ]
    for copy in stores:
        copy.start()

    direct(moves - 1).wait_recv()
    for chunk in range(CHUNKS):
        hop(3, chunk, moves - 1).wait_recv()
    last = pltpu.make_async_copy(held.at[moves + 1], blocks_out.at[1], load_sem.at[1])
    last.start()

    def drain(t, carry):
        direct(t).wait_send()
        for number in (1, 2, 3):
            for chunk in range(CHUNKS):
                hop(number, chunk, t).wait_send()
        return carry

    lax.fori_loop(0, moves, drain, 0)
    for copy in stores:
        copy.wait()
    last.wait()


def last_kernel(
    visit,
    slot,
    users_ref,
    blocks_ref,
    ratings_ref,
    rows_ref,
    cols_ref,
    count_ref,
    users_out,
    items_out,
    users,
    items,
    ratings,
    sems,
):
    users_in = pltpu.make_async_copy(users_ref, users, sems.at[0])
    items_in = pltpu.make_async_copy(blocks_ref.at[slot], items, sems.at[1])
    ratings_in = pltpu.make_async_copy(ratings_ref.at[0, visit, slot], ratings, sems.at[2])
    rest = pltpu.make_async_copy(blocks_ref.at[0], items_out.at[0, 0], sems.at[3])
    for copy in (users_in, items_in, ratings_in, rest):
        copy.start()
    for copy in (users_in, items_in, ratings_in):
        copy.wait()

    def one(k, carry):
        a, c = rows_ref[0, visit, slot, k], cols_ref[0, visit, slot, k]
        users[a], items[c] = tile_update(users[a], items[c], ratings[k])
        return carry

    lax.fori_loop(0, count_ref[0, slot, visit], one, 0)

    users_back = pltpu.make_async_copy(users, users_out, sems.at[0])
    items_back = pltpu.make_async_copy(items, items_out.at[0, slot], sems.at[1])
    users_back.start()
    items_back.start()
    rest.wait()
    users_back.wait()
    items_back.wait()


def body(n_wide, n_narrow, user_factors, item_factors, tile_rows, tile_cols, tile_count, ratings):
    visits, slots, most = tile_rows.shape[1:]
    steps = visits * slots
    moves = steps - slots
    rank = user_factors.shape[1]
    user_tiles = user_factors.shape[0] // TILE
    user_blocks = user_factors.reshape(user_tiles, TILE, rank)
    block_rows = item_factors.shape[2]
    anywhere = pl.BlockSpec(memory_space=pl.ANY)
    hbm = pl.BlockSpec(memory_space=pltpu.HBM)
    smem = pl.BlockSpec(memory_space=pltpu.SMEM)
    f32 = jnp.float32
    tables = (tile_rows, tile_cols, tile_count.swapaxes(1, 2))
    shape = jax.ShapeDtypeStruct
    users_then, blocks_then = pl.pallas_call(
        functools.partial(kernel, n_wide, n_narrow, visits, slots, most),
        out_shape=(
            shape(user_blocks.shape, f32),
            shape(item_factors.shape[1:], f32),
        ),
        in_specs=[hbm, hbm, hbm, smem, smem, smem],
        out_specs=(anywhere, anywhere),
        scratch_shapes=[
            pltpu.VMEM((user_tiles + most, TILE, rank), f32),
            pltpu.VMEM((block_rows // TILE + most, TILE, rank), f32),
            pltpu.VMEM((steps, block_rows, rank), f32),
            pltpu.VMEM((moves, CHUNKS, CHUNK_ROWS, rank), f32),
            pltpu.VMEM((moves, CHUNKS, CHUNK_ROWS, rank), f32),
            pltpu.VMEM((moves + 1, most, TILE, TILE), ratings.dtype),
            pltpu.SemaphoreType.DMA((3,)),
            pltpu.SemaphoreType.DMA((moves + 1,)),
            pltpu.SemaphoreType.DMA((1 + 3 * CHUNKS, moves)),
            pltpu.SemaphoreType.DMA((1 + 3 * CHUNKS, moves)),
        ],
        compiler_params=pltpu.CompilerParams(
            collective_id=0, has_side_effects=True, vmem_limit_bytes=VMEM_GRANT
        ),
        name="sgd_sweep",
    )(user_blocks, item_factors, ratings, *tables)
    item_tiles = block_rows // TILE
    users_new, items_new = pl.pallas_call(
        functools.partial(last_kernel, visits - 1, slots - 1),
        out_shape=(
            shape(user_blocks.shape, f32),
            shape((1, slots, item_tiles, TILE, rank), f32),
        ),
        in_specs=[anywhere, anywhere, hbm, smem, smem, smem],
        out_specs=(anywhere, anywhere),
        scratch_shapes=[
            pltpu.VMEM(user_blocks.shape, f32),
            pltpu.VMEM((item_tiles, TILE, rank), f32),
            pltpu.VMEM((most, TILE, TILE), ratings.dtype),
            pltpu.SemaphoreType.DMA((4,)),
        ],
        compiler_params=pltpu.CompilerParams(vmem_limit_bytes=VMEM_GRANT),
        name="last_slot",
    )(users_then, blocks_then.reshape(slots, item_tiles, TILE, rank), ratings, *tables)
    return users_new.reshape(user_factors.shape), items_new.reshape(item_factors.shape)


def solution(mesh):
    both = ("wide", "narrow")
    in_specs = (
        P(both, None),
        P(both, None, None, None),
        P(both, None, None, None),
        P(both, None, None, None),
        P(both, None, None),
        P(both, None, None, None, None, None),
    )
    out_specs = (P(both, None), P(both, None, None, None))
    run = functools.partial(body, mesh.shape["wide"], mesh.shape["narrow"])
    return jax.shard_map(run, mesh=mesh, in_specs=in_specs, out_specs=out_specs, check_vma=False)
```

```python
import functools

import jax
import jax.numpy as jnp
from jax import lax
from jax.experimental import pallas as pl
from jax.experimental.pallas import tpu as pltpu
from jax.sharding import PartitionSpec as P

learn_rate = 0.0035
decay_weight = 0.05

RING = 4
TILE = 128
RELAY_ROWS = 128
VMEM_GRANT = 56 << 20
CHUNKS = 2
LAST_RELAY_ROWS = 96
FORWARDS = ((0, 2, 0), (2, 2, 1), (4, 3, 0), (8, 3, 1))
MESH = pl.DeviceIdType.MESH


def split(x):
    high = x.astype(jnp.bfloat16)
    return high, (x - high.astype(jnp.float32)).astype(jnp.bfloat16)


def step_of(products, rating):
    t = TILE
    errors = (products[:t, :t] + (products[:t, t:] + products[t:, :t])) - rating
    return errors * -learn_rate


def tile_update(users, items, rating):
    uh, ul = split(users)
    ih, il = split(items)
    rating = rating.astype(jnp.float32)
    u_both, i_both = jnp.concatenate([uh, ul], 0), jnp.concatenate([ih, il], 0)
    rows_by_rows = (((1,), (1,)), ((), ()))
    f32 = jnp.float32
    s = lax.dot_general(u_both, i_both, rows_by_rows, preferred_element_type=f32)
    s_turned = lax.dot_general(i_both, u_both, rows_by_rows, preferred_element_type=f32)
    eh, el = split(step_of(s, rating))
    th, tl = split(step_of(s_turned, rating.T))
    user_step = jnp.dot(
        jnp.concatenate([eh, el, eh], 1),
        jnp.concatenate([ih, ih, il], 0),
        preferred_element_type=f32,
    )
    item_step = jnp.dot(
        jnp.concatenate([th, tl, th], 1),
        jnp.concatenate([uh, uh, ul], 0),
        preferred_element_type=f32,
    )
    keep = 1.0 - learn_rate * decay_weight
    return users * keep + user_step, items * keep + item_step


def pick(values, index):
    out = values[0]
    for i in range(1, len(values)):
        out = jnp.where(index == i, values[i], out)
    return out


def kernel(
    n_wide,
    n_narrow,
    visits,
    slots,
    most,
    users_ref,
    items_ref,
    ratings_ref,
    rows_ref,
    cols_ref,
    count_ref,
    users_out,
    blocks_out,
    users,
    work,
    held,
    relay_one,
    relay_two,
    ratings,
    load_sem,
    rating_sem,
    send_sem,
    recv_sem,
):
    steps = visits * slots
    moves = steps - slots
    user_tiles = users_ref.shape[0]
    block_rows = items_ref.shape[2]
    item_tiles = block_rows // TILE

    w = lax.axis_index("wide")
    n = lax.axis_index("narrow")
    y = lax.rem(w, RING)
    base = w - y
    after = lax.rem(w + 1, n_wide)
    before = lax.rem(w + n_wide - 1, n_wide)
    down = base + lax.rem(y + RING - 1, RING)
    up = base + lax.rem(y + 1, RING)
    third_to = lax.rem(down + jnp.where(y == RING - 3, RING, 0), n_wide)
    third_from = lax.rem(up + n_wide - jnp.where(y == 0, RING, 0), n_wide)
    n_after = lax.rem(n + 1, n_narrow)
    n_before = lax.rem(n + n_narrow - 1, n_narrow)

    first = [pltpu.make_async_copy(items_ref.at[0, 0], held.at[0], load_sem.at[0])]
    for i in range(user_tiles // 2):
        two = pl.ds(2 * i, 2)
        first.append(pltpu.make_async_copy(users_ref.at[two], users.at[two], load_sem.at[2 + i]))
    second = pltpu.make_async_copy(items_ref.at[0, 1], held.at[1], load_sem.at[1])

    def rating_copy(t):
        return pltpu.make_async_copy(
            ratings_ref.at[0, t // slots, lax.rem(t, slots)], ratings.at[t], rating_sem.at[t]
        )

    for copy in first:
        copy.start()
    rating_copy(0).start()
    barrier = pltpu.get_barrier_semaphore()
    partners = [
        (after, n),
        (before, n),
        (down, n),
        (up, n),
        (third_to, n),
        (third_from, n),
        (after, n_after),
        (before, n_before),
        (third_to, n_after),
        (third_from, n_before),
    ]
    for partner in partners:
        pl.semaphore_signal(barrier, inc=1, device_id=partner, device_id_type=MESH)
    pl.semaphore_wait(barrier, len(partners))

    def remote(kind, t, src, dst, device):
        return pltpu.make_async_remote_copy(
            src_ref=src,
            dst_ref=dst,
            send_sem=send_sem.at[kind, t],
            recv_sem=recv_sem.at[kind, t],
            device_id=device,
            device_id_type=MESH,
        )

    def ending_n(t):
        return jnp.where(t >= moves - slots, n_after, n)

    def direct(t, relayed=RELAY_ROWS):
        rows = pl.ds(0, block_rows - relayed)
        return remote(0, t, held.at[t, rows], held.at[t + slots, rows], (after, ending_n(t)))

    def hop(number, chunk, t, relayed=RELAY_ROWS):
        kind = 1 + (number - 1) * CHUNKS + chunk
        size = relayed // CHUNKS
        rows = pl.ds(block_rows - relayed + chunk * size, size)
        part = pl.ds(0, size)
        if number == 1:
            src, dst, device = held.at[t, rows], relay_one.at[t, chunk, part], (down, n)
        elif number == 2:
            src, dst, device = relay_one.at[t, chunk, part], relay_two.at[t, chunk, part], (down, n)
        else:
            src, dst = relay_two.at[t, chunk, part], held.at[t + slots, rows]
            device = (third_to, ending_n(t))
        return remote(kind, t, src, dst, device)

    for copy in first:
        copy.wait()
    second.start()
    for t in range(1, moves + 1):
        rating_copy(t).start()

    def step(t, carry):
        visit, slot = t // slots, lax.rem(t, slots)
        count = count_ref[0, slot, visit]

        @pl.when(t == 1)
        def _():
            second.wait()

        rating_copy(t).wait()

        @pl.when(t >= slots)
        def _():
            direct(t - slots).wait_recv()
            for chunk in range(CHUNKS):
                hop(3, chunk, t - slots).wait_recv()

        for i in range(item_tiles):
            work[i] = held[t, i * TILE : (i + 1) * TILE, :]

        def one(k, state):
            user_at, item_at = state
            live = k < count
            a = jnp.where(live, rows_ref[0, visit, slot, k], 0)
            c = jnp.where(live, cols_ref[0, visit, slot, k], 0)
            ua = pick(user_at, a)
            ia = pick(item_at, c)
            new_users, new_items = tile_update(
                users[ua],
                work[ia],
                ratings[t, k],
            )
            users[user_tiles + k] = new_users
            work[item_tiles + k] = new_items
            user_at = tuple(
                jnp.where(live & (a == i), user_tiles + k, v) for i, v in enumerate(user_at)
            )
            item_at = tuple(
                jnp.where(live & (c == i), item_tiles + k, v) for i, v in enumerate(item_at)
            )
            return user_at, item_at

        state = (
            tuple(jnp.int32(i) for i in range(user_tiles)),
            tuple(jnp.int32(i) for i in range(item_tiles)),
        )
        done = 0
        for position, number, chunk in FORWARDS:
            if position > done:
                state = lax.fori_loop(done, position, one, state, unroll=2)
                done = position

            @pl.when((t >= 1) & (t < moves))
            def _():
                hop(number - 1, chunk, t - 1).wait_recv()
                hop(number, chunk, t - 1).start()

            @pl.when(t == moves)
            def _():
                hop(number - 1, chunk, moves - 1, LAST_RELAY_ROWS).wait_recv()
                hop(number, chunk, moves - 1, LAST_RELAY_ROWS).start()

        if done < most:
            state = lax.fori_loop(done, most, one, state, unroll=2)
        user_at, item_at = state

        for i in range(item_tiles):
            held[t, i * TILE : (i + 1) * TILE, :] = work[item_at[i]]

        @pl.when(t < moves - 1)
        def _():
            for chunk in range(CHUNKS):
                hop(1, chunk, t).start()
            direct(t).start()

        @pl.when(t == moves - 1)
        def _():
            for chunk in range(CHUNKS):
                hop(1, chunk, moves - 1, LAST_RELAY_ROWS).start()
            direct(moves - 1, LAST_RELAY_ROWS).start()

        for i in range(user_tiles):
            users[i] = users[user_at[i]]

        return carry

    lax.fori_loop(0, moves + 1, step, 0)

    stores = [
        pltpu.make_async_copy(users.at[pl.ds(0, user_tiles)], users_out, load_sem.at[2]),
        pltpu.make_async_copy(held.at[moves], blocks_out.at[0], load_sem.at[0]),
    ]
    for copy in stores:
        copy.start()

    direct(moves - 1, LAST_RELAY_ROWS).wait_recv()
    for chunk in range(CHUNKS):
        hop(3, chunk, moves - 1, LAST_RELAY_ROWS).wait_recv()
    last = pltpu.make_async_copy(held.at[moves + 1], blocks_out.at[1], load_sem.at[1])
    last.start()

    def drain(t, carry):
        direct(t).wait_send()
        for number in (1, 2, 3):
            for chunk in range(CHUNKS):
                hop(number, chunk, t).wait_send()
        return carry

    lax.fori_loop(0, moves - 1, drain, 0)
    direct(moves - 1, LAST_RELAY_ROWS).wait_send()
    for number in (1, 2, 3):
        for chunk in range(CHUNKS):
            hop(number, chunk, moves - 1, LAST_RELAY_ROWS).wait_send()
    for copy in stores:
        copy.wait()
    last.wait()


def last_kernel(
    visit,
    slot,
    users_ref,
    blocks_ref,
    ratings_ref,
    rows_ref,
    cols_ref,
    count_ref,
    users_out,
    items_out,
    users,
    items,
    others,
    ratings,
    sems,
    user_sems,
    item_sems,
):
    user_tiles, item_tiles = users.shape[0], items.shape[0]
    most = ratings.shape[0]
    pieces = user_tiles // 2
    copies = [
        pltpu.make_async_copy(blocks_ref.at[slot], items, sems.at[0]),
        pltpu.make_async_copy(ratings_ref.at[0, visit, slot], ratings, sems.at[1]),
    ]
    for i in range(pieces):
        two = pl.ds(2 * i, 2)
        copies.append(pltpu.make_async_copy(users_ref.at[two], users.at[two], sems.at[3 + i]))
    rest_in = pltpu.make_async_copy(blocks_ref.at[0], others, sems.at[2])
    for copy in copies:
        copy.start()
    rest_in.start()

    def user_back(i):
        return pltpu.make_async_copy(users.at[i], users_out.at[i], user_sems.at[i])

    def item_back(i):
        return pltpu.make_async_copy(items.at[i], items_out.at[0, slot, i], item_sems.at[i])

    count = count_ref[0, slot, visit]

    def later(table, index, start):
        found = jnp.int32(0)
        for k in range(most):
            same = (table[0, visit, slot, k] == index) & (k < count) & (k >= start)
            found = jnp.where(same, 1, found)
        return found == 1

    for copy in copies:
        copy.wait()
    for table, tiles, back in ((rows_ref, user_tiles, user_back), (cols_ref, item_tiles, item_back)):
        for i in range(tiles):

            @pl.when(jnp.logical_not(later(table, i, 0)))
            def _():
                back(i).start()

    rest_in.wait()
    rest_back = pltpu.make_async_copy(others, items_out.at[0, 0], sems.at[2])
    rest_back.start()

    def one(k, carry):
        a, c = rows_ref[0, visit, slot, k], cols_ref[0, visit, slot, k]
        users[a], items[c] = tile_update(users[a], items[c], ratings[k])

        @pl.when(jnp.logical_not(later(rows_ref, a, k + 1)))
        def _():
            user_back(a).start()

        @pl.when(jnp.logical_not(later(cols_ref, c, k + 1)))
        def _():
            item_back(c).start()

        return carry

    lax.fori_loop(0, count, one, 0)

    rest_back.wait()
    for i in range(user_tiles):
        user_back(i).wait()
    for i in range(item_tiles):
        item_back(i).wait()


def body(n_wide, n_narrow, user_factors, item_factors, tile_rows, tile_cols, tile_count, ratings):
    visits, slots, most = tile_rows.shape[1:]
    steps = visits * slots
    moves = steps - slots
    rank = user_factors.shape[1]
    user_tiles = user_factors.shape[0] // TILE
    user_blocks = user_factors.reshape(user_tiles, TILE, rank)
    block_rows = item_factors.shape[2]
    anywhere = pl.BlockSpec(memory_space=pl.ANY)
    hbm = pl.BlockSpec(memory_space=pltpu.HBM)
    smem = pl.BlockSpec(memory_space=pltpu.SMEM)
    f32 = jnp.float32
    tables = (tile_rows, tile_cols, tile_count.swapaxes(1, 2))
    shape = jax.ShapeDtypeStruct
    item_tiles = block_rows // TILE
    users_then, blocks_then = pl.pallas_call(
        functools.partial(kernel, n_wide, n_narrow, visits, slots, most),
        out_shape=(
            shape(user_blocks.shape, f32),
            shape(item_factors.shape[1:], f32),
        ),
        in_specs=[hbm, hbm, hbm, smem, smem, smem],
        out_specs=(anywhere, anywhere),
        scratch_shapes=[
            pltpu.VMEM((user_tiles + most, TILE, rank), f32),
            pltpu.VMEM((block_rows // TILE + most, TILE, rank), f32),
            pltpu.VMEM((steps, block_rows, rank), f32),
            pltpu.VMEM((moves, CHUNKS, RELAY_ROWS // CHUNKS, rank), f32),
            pltpu.VMEM((moves, CHUNKS, RELAY_ROWS // CHUNKS, rank), f32),
            pltpu.VMEM((moves + 1, most, TILE, TILE), ratings.dtype),
            pltpu.SemaphoreType.DMA((2 + user_tiles // 2,)),
            pltpu.SemaphoreType.DMA((moves + 1,)),
            pltpu.SemaphoreType.DMA((1 + 3 * CHUNKS, moves)),
            pltpu.SemaphoreType.DMA((1 + 3 * CHUNKS, moves)),
        ],
        compiler_params=pltpu.CompilerParams(
            collective_id=0, has_side_effects=True, vmem_limit_bytes=VMEM_GRANT
        ),
        name="sgd_sweep",
    )(user_blocks, item_factors, ratings, *tables)
    users_new, items_new = pl.pallas_call(
        functools.partial(last_kernel, visits - 1, slots - 1),
        out_shape=(
            shape(user_blocks.shape, f32),
            shape((1, slots, item_tiles, TILE, rank), f32),
        ),
        in_specs=[anywhere, anywhere, hbm, smem, smem, smem],
        out_specs=(anywhere, anywhere),
        scratch_shapes=[
            pltpu.VMEM(user_blocks.shape, f32),
            pltpu.VMEM((item_tiles, TILE, rank), f32),
            pltpu.VMEM((item_tiles, TILE, rank), f32),
            pltpu.VMEM((most, TILE, TILE), ratings.dtype),
            pltpu.SemaphoreType.DMA((3 + user_tiles // 2,)),
            pltpu.SemaphoreType.DMA((user_tiles,)),
            pltpu.SemaphoreType.DMA((item_tiles,)),
        ],
        compiler_params=pltpu.CompilerParams(vmem_limit_bytes=VMEM_GRANT),
        name="last_slot",
    )(users_then, blocks_then.reshape(slots, item_tiles, TILE, rank), ratings, *tables)
    return users_new.reshape(user_factors.shape), items_new.reshape(item_factors.shape)


def solution(mesh):
    both = ("wide", "narrow")
    in_specs = (
        P(both, None),
        P(both, None, None, None),
        P(both, None, None, None),
        P(both, None, None, None),
        P(both, None, None),
        P(both, None, None, None, None, None),
    )
    out_specs = (P(both, None), P(both, None, None, None))
    run = functools.partial(body, mesh.shape["wide"], mesh.shape["narrow"])
    return jax.shard_map(run, mesh=mesh, in_specs=in_specs, out_specs=out_specs, check_vma=False)
```

```python
import functools

import jax
import jax.numpy as jnp
from jax import lax
from jax.experimental import pallas as pl
from jax.experimental.pallas import tpu as pltpu
from jax.sharding import PartitionSpec as P

learn_rate = 0.0035
decay_weight = 0.05

RING = 4
TILE = 128
RELAY_ROWS = 128
VMEM_GRANT = 56 << 20
CHUNKS = 2
LAST_RELAY_ROWS = 96
FORWARDS = ((0, 2, 0), (2, 2, 1), (4, 3, 0), (8, 3, 1))
MESH = pl.DeviceIdType.MESH


def split(x):
    high = x.astype(jnp.bfloat16)
    return high, (x - high.astype(jnp.float32)).astype(jnp.bfloat16)


def step_of(products, rating):
    t = TILE
    errors = (products[:t, :t] + (products[:t, t:] + products[t:, :t])) - rating
    return errors * -learn_rate


def tile_update(users, items, rating):
    uh, ul = split(users)
    ih, il = split(items)
    rating = rating.astype(jnp.float32)
    u_both, i_both = jnp.concatenate([uh, ul], 0), jnp.concatenate([ih, il], 0)
    rows_by_rows = (((1,), (1,)), ((), ()))
    f32 = jnp.float32
    s = lax.dot_general(u_both, i_both, rows_by_rows, preferred_element_type=f32)
    s_turned = lax.dot_general(i_both, u_both, rows_by_rows, preferred_element_type=f32)
    eh, el = split(step_of(s, rating))
    th, tl = split(step_of(s_turned, rating.T))
    user_step = jnp.dot(
        jnp.concatenate([eh, el, eh], 1),
        jnp.concatenate([ih, ih, il], 0),
        preferred_element_type=f32,
    )
    item_step = jnp.dot(
        jnp.concatenate([th, tl, th], 1),
        jnp.concatenate([uh, uh, ul], 0),
        preferred_element_type=f32,
    )
    keep = 1.0 - learn_rate * decay_weight
    return users * keep + user_step, items * keep + item_step


def pick(values, index):
    out = values[0]
    for i in range(1, len(values)):
        out = jnp.where(index == i, values[i], out)
    return out


def kernel(
    n_wide,
    n_narrow,
    visits,
    slots,
    most,
    users_ref,
    items_ref,
    ratings_ref,
    rows_ref,
    cols_ref,
    count_ref,
    users_out,
    blocks_out,
    users,
    work,
    held,
    relay_one,
    relay_two,
    ratings,
    load_sem,
    rating_sem,
    send_sem,
    recv_sem,
):
    steps = visits * slots
    moves = steps - slots
    user_tiles = users_ref.shape[0]
    block_rows = items_ref.shape[2]
    item_tiles = block_rows // TILE

    w = lax.axis_index("wide")
    n = lax.axis_index("narrow")
    y = lax.rem(w, RING)
    base = w - y
    after = lax.rem(w + 1, n_wide)
    before = lax.rem(w + n_wide - 1, n_wide)
    down = base + lax.rem(y + RING - 1, RING)
    up = base + lax.rem(y + 1, RING)
    third_to = lax.rem(down + jnp.where(y == RING - 3, RING, 0), n_wide)
    third_from = lax.rem(up + n_wide - jnp.where(y == 0, RING, 0), n_wide)
    n_after = lax.rem(n + 1, n_narrow)
    n_before = lax.rem(n + n_narrow - 1, n_narrow)

    first = [pltpu.make_async_copy(items_ref.at[0, 0], held.at[0], load_sem.at[0])]
    for i in range(user_tiles // 2):
        two = pl.ds(2 * i, 2)
        first.append(pltpu.make_async_copy(users_ref.at[two], users.at[two], load_sem.at[2 + i]))
    second = pltpu.make_async_copy(items_ref.at[0, 1], held.at[1], load_sem.at[1])

    def rating_copy(t):
        return pltpu.make_async_copy(
            ratings_ref.at[0, t // slots, lax.rem(t, slots)], ratings.at[t], rating_sem.at[t]
        )

    for copy in first:
        copy.start()
    rating_copy(0).start()
    barrier = pltpu.get_barrier_semaphore()
    partners = [
        (after, n),
        (before, n),
        (down, n),
        (up, n),
        (third_to, n),
        (third_from, n),
        (after, n_after),
        (before, n_before),
        (third_to, n_after),
        (third_from, n_before),
    ]
    for partner in partners:
        pl.semaphore_signal(barrier, inc=1, device_id=partner, device_id_type=MESH)
    pl.semaphore_wait(barrier, len(partners))

    def remote(kind, t, src, dst, device):
        return pltpu.make_async_remote_copy(
            src_ref=src,
            dst_ref=dst,
            send_sem=send_sem.at[kind, t],
            recv_sem=recv_sem.at[kind, t],
            device_id=device,
            device_id_type=MESH,
        )

    def ending_n(t):
        return jnp.where(t >= moves - slots, n_after, n)

    def direct(t, relayed=RELAY_ROWS):
        rows = pl.ds(0, block_rows - relayed)
        return remote(0, t, held.at[t, rows], held.at[t + slots, rows], (after, ending_n(t)))

    def hop(number, chunk, t, relayed=RELAY_ROWS):
        kind = 1 + (number - 1) * CHUNKS + chunk
        size = relayed // CHUNKS
        rows = pl.ds(block_rows - relayed + chunk * size, size)
        part = pl.ds(0, size)
        if number == 1:
            src, dst, device = held.at[t, rows], relay_one.at[t, chunk, part], (down, n)
        elif number == 2:
            src, dst, device = relay_one.at[t, chunk, part], relay_two.at[t, chunk, part], (down, n)
        else:
            src, dst = relay_two.at[t, chunk, part], held.at[t + slots, rows]
            device = (third_to, ending_n(t))
        return remote(kind, t, src, dst, device)

    for copy in first:
        copy.wait()
    second.start()
    for t in range(1, moves + 1):
        rating_copy(t).start()

    def step(t, carry):
        visit, slot = t // slots, lax.rem(t, slots)
        count = count_ref[0, slot, visit]

        @pl.when(t == 1)
        def _():
            second.wait()

        rating_copy(t).wait()

        @pl.when(t >= slots)
        def _():
            direct(t - slots).wait_recv()
            for chunk in range(CHUNKS):
                hop(3, chunk, t - slots).wait_recv()

        for i in range(item_tiles):
            work[i] = held[t, i * TILE : (i + 1) * TILE, :]

        def one(k, state):
            user_at, item_at = state
            live = k < count
            a = jnp.where(live, rows_ref[0, visit, slot, k], 0)
            c = jnp.where(live, cols_ref[0, visit, slot, k], 0)
            ua = pick(user_at, a)
            ia = pick(item_at, c)
            new_users, new_items = tile_update(
                users[ua],
                work[ia],
                ratings[t, k],
            )
            users[user_tiles + k] = new_users
            work[item_tiles + k] = new_items
            user_at = tuple(
                jnp.where(live & (a == i), user_tiles + k, v) for i, v in enumerate(user_at)
            )
            item_at = tuple(
                jnp.where(live & (c == i), item_tiles + k, v) for i, v in enumerate(item_at)
            )
            return user_at, item_at

        state = (
            tuple(jnp.int32(i) for i in range(user_tiles)),
            tuple(jnp.int32(i) for i in range(item_tiles)),
        )
        done = 0
        for position, number, chunk in FORWARDS:
            if position > done:
                state = lax.fori_loop(done, position, one, state, unroll=2)
                done = position

            @pl.when((t >= 1) & (t < moves))
            def _():
                hop(number - 1, chunk, t - 1).wait_recv()
                hop(number, chunk, t - 1).start()

            @pl.when(t == moves)
            def _():
                hop(number - 1, chunk, moves - 1, LAST_RELAY_ROWS).wait_recv()
                hop(number, chunk, moves - 1, LAST_RELAY_ROWS).start()

        if done < most:
            state = lax.fori_loop(done, most, one, state, unroll=2)
        user_at, item_at = state

        for i in range(item_tiles):
            held[t, i * TILE : (i + 1) * TILE, :] = work[item_at[i]]

        @pl.when(t < moves - 1)
        def _():
            for chunk in range(CHUNKS):
                hop(1, chunk, t).start()
            direct(t).start()

        @pl.when(t == moves - 1)
        def _():
            for chunk in range(CHUNKS):
                hop(1, chunk, moves - 1, LAST_RELAY_ROWS).start()
            direct(moves - 1, LAST_RELAY_ROWS).start()

        for i in range(user_tiles):
            users[i] = users[user_at[i]]

        return carry

    lax.fori_loop(0, moves + 1, step, 0)

    stores = [
        pltpu.make_async_copy(users.at[pl.ds(0, user_tiles)], users_out, load_sem.at[2]),
        pltpu.make_async_copy(held.at[moves], blocks_out.at[0], load_sem.at[0]),
    ]
    for copy in stores:
        copy.start()

    def drain(t, carry):
        direct(t).wait_send()
        for number in (1, 2, 3):
            for chunk in range(CHUNKS):
                hop(number, chunk, t).wait_send()
        return carry

    lax.fori_loop(0, moves - 1, drain, 0)
    for copy in stores:
        copy.wait()

    direct(moves - 1, LAST_RELAY_ROWS).wait_recv()
    for chunk in range(CHUNKS):
        hop(3, chunk, moves - 1, LAST_RELAY_ROWS).wait_recv()
    last = pltpu.make_async_copy(held.at[moves + 1], blocks_out.at[1], load_sem.at[1])
    last.start()
    direct(moves - 1, LAST_RELAY_ROWS).wait_send()
    for number in (1, 2, 3):
        for chunk in range(CHUNKS):
            hop(number, chunk, moves - 1, LAST_RELAY_ROWS).wait_send()
    last.wait()


def last_kernel(
    visit,
    slot,
    users_ref,
    blocks_ref,
    ratings_ref,
    rows_ref,
    cols_ref,
    count_ref,
    users_out,
    items_out,
    users,
    items,
    others,
    ratings,
    sems,
    user_sems,
    item_sems,
):
    user_tiles, item_tiles = users.shape[0], items.shape[0]
    most = ratings.shape[0]
    pieces = user_tiles // 2
    copies = [
        pltpu.make_async_copy(blocks_ref.at[slot], items, sems.at[0]),
        pltpu.make_async_copy(ratings_ref.at[0, visit, slot], ratings, sems.at[1]),
    ]
    for i in range(pieces):
        two = pl.ds(2 * i, 2)
        copies.append(pltpu.make_async_copy(users_ref.at[two], users.at[two], sems.at[3 + i]))
    rest_in = pltpu.make_async_copy(blocks_ref.at[0], others, sems.at[2])
    for copy in copies:
        copy.start()
    rest_in.start()

    def user_back(i):
        return pltpu.make_async_copy(users.at[i], users_out.at[i], user_sems.at[i])

    def item_back(i):
        return pltpu.make_async_copy(items.at[i], items_out.at[0, slot, i], item_sems.at[i])

    count = count_ref[0, slot, visit]

    def later(table, index, start):
        found = jnp.int32(0)
        for k in range(most):
            same = (table[0, visit, slot, k] == index) & (k < count) & (k >= start)
            found = jnp.where(same, 1, found)
        return found == 1

    for copy in copies:
        copy.wait()
    for table, tiles, back in ((rows_ref, user_tiles, user_back), (cols_ref, item_tiles, item_back)):
        for i in range(tiles):

            @pl.when(jnp.logical_not(later(table, i, 0)))
            def _():
                back(i).start()

    rest_in.wait()
    rest_back = pltpu.make_async_copy(others, items_out.at[0, 0], sems.at[2])
    rest_back.start()

    def one(k, carry):
        a, c = rows_ref[0, visit, slot, k], cols_ref[0, visit, slot, k]
        users[a], items[c] = tile_update(users[a], items[c], ratings[k])

        @pl.when(jnp.logical_not(later(rows_ref, a, k + 1)))
        def _():
            user_back(a).start()

        @pl.when(jnp.logical_not(later(cols_ref, c, k + 1)))
        def _():
            item_back(c).start()

        return carry

    lax.fori_loop(0, count, one, 0)

    rest_back.wait()
    for i in range(user_tiles):
        user_back(i).wait()
    for i in range(item_tiles):
        item_back(i).wait()


def body(n_wide, n_narrow, user_factors, item_factors, tile_rows, tile_cols, tile_count, ratings):
    visits, slots, most = tile_rows.shape[1:]
    steps = visits * slots
    moves = steps - slots
    rank = user_factors.shape[1]
    user_tiles = user_factors.shape[0] // TILE
    user_blocks = user_factors.reshape(user_tiles, TILE, rank)
    block_rows = item_factors.shape[2]
    anywhere = pl.BlockSpec(memory_space=pl.ANY)
    hbm = pl.BlockSpec(memory_space=pltpu.HBM)
    smem = pl.BlockSpec(memory_space=pltpu.SMEM)
    f32 = jnp.float32
    tables = (tile_rows, tile_cols, tile_count.swapaxes(1, 2))
    shape = jax.ShapeDtypeStruct
    item_tiles = block_rows // TILE
    users_then, blocks_then = pl.pallas_call(
        functools.partial(kernel, n_wide, n_narrow, visits, slots, most),
        out_shape=(
            shape(user_blocks.shape, f32),
            shape(item_factors.shape[1:], f32),
        ),
        in_specs=[hbm, hbm, hbm, smem, smem, smem],
        out_specs=(anywhere, anywhere),
        scratch_shapes=[
            pltpu.VMEM((user_tiles + most, TILE, rank), f32),
            pltpu.VMEM((block_rows // TILE + most, TILE, rank), f32),
            pltpu.VMEM((steps, block_rows, rank), f32),
            pltpu.VMEM((moves, CHUNKS, RELAY_ROWS // CHUNKS, rank), f32),
            pltpu.VMEM((moves, CHUNKS, RELAY_ROWS // CHUNKS, rank), f32),
            pltpu.VMEM((moves + 1, most, TILE, TILE), ratings.dtype),
            pltpu.SemaphoreType.DMA((2 + user_tiles // 2,)),
            pltpu.SemaphoreType.DMA((moves + 1,)),
            pltpu.SemaphoreType.DMA((1 + 3 * CHUNKS, moves)),
            pltpu.SemaphoreType.DMA((1 + 3 * CHUNKS, moves)),
        ],
        compiler_params=pltpu.CompilerParams(
            collective_id=0, has_side_effects=True, vmem_limit_bytes=VMEM_GRANT
        ),
        name="sgd_sweep",
    )(user_blocks, item_factors, ratings, *tables)
    users_new, items_new = pl.pallas_call(
        functools.partial(last_kernel, visits - 1, slots - 1),
        out_shape=(
            shape(user_blocks.shape, f32),
            shape((1, slots, item_tiles, TILE, rank), f32),
        ),
        in_specs=[anywhere, anywhere, hbm, smem, smem, smem],
        out_specs=(anywhere, anywhere),
        scratch_shapes=[
            pltpu.VMEM(user_blocks.shape, f32),
            pltpu.VMEM((item_tiles, TILE, rank), f32),
            pltpu.VMEM((item_tiles, TILE, rank), f32),
            pltpu.VMEM((most, TILE, TILE), ratings.dtype),
            pltpu.SemaphoreType.DMA((3 + user_tiles // 2,)),
            pltpu.SemaphoreType.DMA((user_tiles,)),
            pltpu.SemaphoreType.DMA((item_tiles,)),
        ],
        compiler_params=pltpu.CompilerParams(vmem_limit_bytes=VMEM_GRANT),
        name="last_slot",
    )(users_then, blocks_then.reshape(slots, item_tiles, TILE, rank), ratings, *tables)
    return users_new.reshape(user_factors.shape), items_new.reshape(item_factors.shape)


def solution(mesh):
    both = ("wide", "narrow")
    in_specs = (
        P(both, None),
        P(both, None, None, None),
        P(both, None, None, None),
        P(both, None, None, None),
        P(both, None, None),
        P(both, None, None, None, None, None),
    )
    out_specs = (P(both, None), P(both, None, None, None))
    run = functools.partial(body, mesh.shape["wide"], mesh.shape["narrow"])
    return jax.shard_map(run, mesh=mesh, in_specs=in_specs, out_specs=out_specs, check_vma=False)
```

```python
import functools

import jax
import jax.numpy as jnp
from jax import lax
from jax.experimental import pallas as pl
from jax.experimental.pallas import tpu as pltpu
from jax.sharding import PartitionSpec as P

learn_rate = 0.0035
decay_weight = 0.05

RING = 4
TILE = 128
RELAY_ROWS = 128
VMEM_GRANT = 48 << 20
CHUNKS = 2
LAST_RELAY_ROWS = 96
FORWARDS = ((0, 2, 0), (2, 2, 1), (4, 3, 0), (8, 3, 1))
MESH = pl.DeviceIdType.MESH


def split(x):
    high = x.astype(jnp.bfloat16)
    return high, (x - high.astype(jnp.float32)).astype(jnp.bfloat16)


def step_of(products, rating):
    t = TILE
    errors = (products[:t, :t] + (products[:t, t:] + products[t:, :t])) - rating
    return errors * -learn_rate


def tile_update(users, items, rating):
    uh, ul = split(users)
    ih, il = split(items)
    rating = rating.astype(jnp.float32)
    u_both, i_both = jnp.concatenate([uh, ul], 0), jnp.concatenate([ih, il], 0)
    rows_by_rows = (((1,), (1,)), ((), ()))
    f32 = jnp.float32
    s = lax.dot_general(u_both, i_both, rows_by_rows, preferred_element_type=f32)
    s_turned = lax.dot_general(i_both, u_both, rows_by_rows, preferred_element_type=f32)
    eh, el = split(step_of(s, rating))
    th, tl = split(step_of(s_turned, rating.T))
    user_step = jnp.dot(
        jnp.concatenate([eh, el, eh], 1),
        jnp.concatenate([ih, ih, il], 0),
        preferred_element_type=f32,
    )
    item_step = jnp.dot(
        jnp.concatenate([th, tl, th], 1),
        jnp.concatenate([uh, uh, ul], 0),
        preferred_element_type=f32,
    )
    keep = 1.0 - learn_rate * decay_weight
    return users * keep + user_step, items * keep + item_step


def pick(values, index):
    out = values[0]
    for i in range(1, len(values)):
        out = jnp.where(index == i, values[i], out)
    return out


def kernel(
    n_wide,
    n_narrow,
    visits,
    slots,
    most,
    users_ref,
    items_ref,
    ratings_ref,
    rows_ref,
    cols_ref,
    count_ref,
    users_out,
    blocks_out,
    users,
    work,
    held,
    relay_one,
    relay_two,
    ratings,
    load_sem,
    rating_sem,
    send_sem,
    recv_sem,
):
    steps = visits * slots
    moves = steps - slots
    user_tiles = users_ref.shape[0]
    block_rows = items_ref.shape[2]
    item_tiles = block_rows // TILE

    w = lax.axis_index("wide")
    n = lax.axis_index("narrow")
    y = lax.rem(w, RING)
    base = w - y
    after = lax.rem(w + 1, n_wide)
    before = lax.rem(w + n_wide - 1, n_wide)
    down = base + lax.rem(y + RING - 1, RING)
    up = base + lax.rem(y + 1, RING)
    third_to = lax.rem(down + jnp.where(y == RING - 3, RING, 0), n_wide)
    third_from = lax.rem(up + n_wide - jnp.where(y == 0, RING, 0), n_wide)
    n_after = lax.rem(n + 1, n_narrow)
    n_before = lax.rem(n + n_narrow - 1, n_narrow)

    first = [pltpu.make_async_copy(items_ref.at[0, 0], held.at[0], load_sem.at[0])]
    for i in range(user_tiles // 2):
        two = pl.ds(2 * i, 2)
        first.append(pltpu.make_async_copy(users_ref.at[two], users.at[two], load_sem.at[2 + i]))
    second = pltpu.make_async_copy(items_ref.at[0, 1], held.at[1], load_sem.at[1])

    def rating_copy(t):
        return pltpu.make_async_copy(
            ratings_ref.at[0, t // slots, lax.rem(t, slots)], ratings.at[t], rating_sem.at[t]
        )

    for copy in first:
        copy.start()
    rating_copy(0).start()
    barrier = pltpu.get_barrier_semaphore()
    partners = [
        (after, n),
        (before, n),
        (down, n),
        (up, n),
        (third_to, n),
        (third_from, n),
        (after, n_after),
        (before, n_before),
        (third_to, n_after),
        (third_from, n_before),
    ]
    for partner in partners:
        pl.semaphore_signal(barrier, inc=1, device_id=partner, device_id_type=MESH)
    pl.semaphore_wait(barrier, len(partners))

    def remote(kind, t, src, dst, device):
        return pltpu.make_async_remote_copy(
            src_ref=src,
            dst_ref=dst,
            send_sem=send_sem.at[kind, t],
            recv_sem=recv_sem.at[kind, t],
            device_id=device,
            device_id_type=MESH,
        )

    def ending_n(t):
        return jnp.where(t >= moves - slots, n_after, n)

    def direct(t, relayed=RELAY_ROWS):
        rows = pl.ds(0, block_rows - relayed)
        return remote(0, t, held.at[t, rows], held.at[t + slots, rows], (after, ending_n(t)))

    def hop(number, chunk, t, relayed=RELAY_ROWS):
        kind = 1 + (number - 1) * CHUNKS + chunk
        size = relayed // CHUNKS
        rows = pl.ds(block_rows - relayed + chunk * size, size)
        part = pl.ds(0, size)
        if number == 1:
            src, dst, device = held.at[t, rows], relay_one.at[t, chunk, part], (down, n)
        elif number == 2:
            src, dst, device = relay_one.at[t, chunk, part], relay_two.at[t, chunk, part], (down, n)
        else:
            src, dst = relay_two.at[t, chunk, part], held.at[t + slots, rows]
            device = (third_to, ending_n(t))
        return remote(kind, t, src, dst, device)

    for copy in first:
        copy.wait()
    second.start()
    for t in range(1, moves + 1):
        rating_copy(t).start()

    def step(t, carry):
        visit, slot = t // slots, lax.rem(t, slots)
        count = count_ref[0, slot, visit]

        @pl.when(t == 1)
        def _():
            second.wait()

        rating_copy(t).wait()

        @pl.when(t >= slots)
        def _():
            direct(t - slots).wait_recv()
            for chunk in range(CHUNKS):
                hop(3, chunk, t - slots).wait_recv()

        for i in range(item_tiles):
            work[i] = held[t, i * TILE : (i + 1) * TILE, :]

        def one(k, state):
            user_at, item_at = state
            live = k < count
            a = jnp.where(live, rows_ref[0, visit, slot, k], 0)
            c = jnp.where(live, cols_ref[0, visit, slot, k], 0)
            ua = pick(user_at, a)
            ia = pick(item_at, c)
            new_users, new_items = tile_update(
                users[ua],
                work[ia],
                ratings[t, k],
            )
            users[user_tiles + k] = new_users
            work[item_tiles + k] = new_items
            user_at = tuple(
                jnp.where(live & (a == i), user_tiles + k, v) for i, v in enumerate(user_at)
            )
            item_at = tuple(
                jnp.where(live & (c == i), item_tiles + k, v) for i, v in enumerate(item_at)
            )
            return user_at, item_at

        state = (
            tuple(jnp.int32(i) for i in range(user_tiles)),
            tuple(jnp.int32(i) for i in range(item_tiles)),
        )
        done = 0
        for position, number, chunk in FORWARDS:
            if position > done:
                state = lax.fori_loop(done, position, one, state, unroll=2)
                done = position

            @pl.when((t >= 1) & (t < moves))
            def _():
                hop(number - 1, chunk, t - 1).wait_recv()
                hop(number, chunk, t - 1).start()

            @pl.when(t == moves)
            def _():
                hop(number - 1, chunk, moves - 1, LAST_RELAY_ROWS).wait_recv()
                hop(number, chunk, moves - 1, LAST_RELAY_ROWS).start()

        if done < most:
            state = lax.fori_loop(done, most, one, state, unroll=2)
        user_at, item_at = state

        for i in range(item_tiles):
            held[t, i * TILE : (i + 1) * TILE, :] = work[item_at[i]]

        @pl.when(t < moves - 1)
        def _():
            for chunk in range(CHUNKS):
                hop(1, chunk, t).start()
            direct(t).start()

        @pl.when(t == moves - 1)
        def _():
            for chunk in range(CHUNKS):
                hop(1, chunk, moves - 1, LAST_RELAY_ROWS).start()
            direct(moves - 1, LAST_RELAY_ROWS).start()

        for i in range(user_tiles):
            users[i] = users[user_at[i]]

        return carry

    lax.fori_loop(0, moves + 1, step, 0)

    stores = [
        pltpu.make_async_copy(users.at[pl.ds(0, user_tiles)], users_out, load_sem.at[2]),
        pltpu.make_async_copy(held.at[moves], blocks_out.at[0], load_sem.at[0]),
    ]
    for copy in stores:
        copy.start()

    def drain(t, carry):
        direct(t).wait_send()
        for number in (1, 2, 3):
            for chunk in range(CHUNKS):
                hop(number, chunk, t).wait_send()
        return carry

    lax.fori_loop(0, moves - 1, drain, 0)
    for copy in stores:
        copy.wait()

    direct(moves - 1, LAST_RELAY_ROWS).wait_recv()
    for chunk in range(CHUNKS):
        hop(3, chunk, moves - 1, LAST_RELAY_ROWS).wait_recv()
    last = pltpu.make_async_copy(held.at[moves + 1], blocks_out.at[1], load_sem.at[1])
    last.start()
    direct(moves - 1, LAST_RELAY_ROWS).wait_send()
    for number in (1, 2, 3):
        for chunk in range(CHUNKS):
            hop(number, chunk, moves - 1, LAST_RELAY_ROWS).wait_send()
    last.wait()


def last_kernel(
    visit,
    slot,
    users_ref,
    blocks_ref,
    ratings_ref,
    rows_ref,
    cols_ref,
    count_ref,
    users_out,
    items_out,
    users,
    items,
    others,
    ratings,
    sems,
    user_sems,
    item_sems,
):
    user_tiles, item_tiles = users.shape[0], items.shape[0]
    most = ratings.shape[0]
    pieces = user_tiles // 2
    copies = [
        pltpu.make_async_copy(blocks_ref.at[slot], items, sems.at[0]),
        pltpu.make_async_copy(ratings_ref.at[0, visit, slot], ratings, sems.at[1]),
    ]
    for i in range(pieces):
        two = pl.ds(2 * i, 2)
        copies.append(pltpu.make_async_copy(users_ref.at[two], users.at[two], sems.at[3 + i]))
    rest_in = pltpu.make_async_copy(blocks_ref.at[0], others, sems.at[2])
    for copy in copies:
        copy.start()
    rest_in.start()

    def user_back(i):
        return pltpu.make_async_copy(users.at[i], users_out.at[i], user_sems.at[i])

    def item_back(i):
        return pltpu.make_async_copy(items.at[i], items_out.at[0, slot, i], item_sems.at[i])

    count = count_ref[0, slot, visit]

    def later(table, index, start):
        found = jnp.int32(0)
        for k in range(most):
            same = (table[0, visit, slot, k] == index) & (k < count) & (k >= start)
            found = jnp.where(same, 1, found)
        return found == 1

    for copy in copies:
        copy.wait()
    for table, tiles, back in ((rows_ref, user_tiles, user_back), (cols_ref, item_tiles, item_back)):
        for i in range(tiles):

            @pl.when(jnp.logical_not(later(table, i, 0)))
            def _():
                back(i).start()

    rest_in.wait()
    rest_back = pltpu.make_async_copy(others, items_out.at[0, 0], sems.at[2])
    rest_back.start()

    def one(k, carry):
        a, c = rows_ref[0, visit, slot, k], cols_ref[0, visit, slot, k]
        users[a], items[c] = tile_update(users[a], items[c], ratings[k])

        @pl.when(jnp.logical_not(later(rows_ref, a, k + 1)))
        def _():
            user_back(a).start()

        @pl.when(jnp.logical_not(later(cols_ref, c, k + 1)))
        def _():
            item_back(c).start()

        return carry

    lax.fori_loop(0, count, one, 0)

    rest_back.wait()
    for i in range(user_tiles):
        user_back(i).wait()
    for i in range(item_tiles):
        item_back(i).wait()


def body(n_wide, n_narrow, user_factors, item_factors, tile_rows, tile_cols, tile_count, ratings):
    visits, slots, most = tile_rows.shape[1:]
    steps = visits * slots
    moves = steps - slots
    rank = user_factors.shape[1]
    user_tiles = user_factors.shape[0] // TILE
    user_blocks = user_factors.reshape(user_tiles, TILE, rank)
    block_rows = item_factors.shape[2]
    anywhere = pl.BlockSpec(memory_space=pl.ANY)
    hbm = pl.BlockSpec(memory_space=pltpu.HBM)
    smem = pl.BlockSpec(memory_space=pltpu.SMEM)
    f32 = jnp.float32
    tables = (tile_rows, tile_cols, tile_count.swapaxes(1, 2))
    shape = jax.ShapeDtypeStruct
    item_tiles = block_rows // TILE
    users_then, blocks_then = pl.pallas_call(
        functools.partial(kernel, n_wide, n_narrow, visits, slots, most),
        out_shape=(
            shape(user_blocks.shape, f32),
            shape(item_factors.shape[1:], f32),
        ),
        in_specs=[hbm, hbm, hbm, smem, smem, smem],
        out_specs=(anywhere, anywhere),
        scratch_shapes=[
            pltpu.VMEM((user_tiles + most, TILE, rank), f32),
            pltpu.VMEM((block_rows // TILE + most, TILE, rank), f32),
            pltpu.VMEM((steps, block_rows, rank), f32),
            pltpu.VMEM((moves, CHUNKS, RELAY_ROWS // CHUNKS, rank), f32),
            pltpu.VMEM((moves, CHUNKS, RELAY_ROWS // CHUNKS, rank), f32),
            pltpu.VMEM((moves + 1, most, TILE, TILE), ratings.dtype),
            pltpu.SemaphoreType.DMA((2 + user_tiles // 2,)),
            pltpu.SemaphoreType.DMA((moves + 1,)),
            pltpu.SemaphoreType.DMA((1 + 3 * CHUNKS, moves)),
            pltpu.SemaphoreType.DMA((1 + 3 * CHUNKS, moves)),
        ],
        compiler_params=pltpu.CompilerParams(
            collective_id=0, has_side_effects=True, vmem_limit_bytes=VMEM_GRANT
        ),
        name="sgd_sweep",
    )(user_blocks, item_factors, ratings, *tables)
    users_new, items_new = pl.pallas_call(
        functools.partial(last_kernel, visits - 1, slots - 1),
        out_shape=(
            shape(user_blocks.shape, f32),
            shape((1, slots, item_tiles, TILE, rank), f32),
        ),
        in_specs=[anywhere, anywhere, hbm, smem, smem, smem],
        out_specs=(anywhere, anywhere),
        scratch_shapes=[
            pltpu.VMEM(user_blocks.shape, f32),
            pltpu.VMEM((item_tiles, TILE, rank), f32),
            pltpu.VMEM((item_tiles, TILE, rank), f32),
            pltpu.VMEM((most, TILE, TILE), ratings.dtype),
            pltpu.SemaphoreType.DMA((3 + user_tiles // 2,)),
            pltpu.SemaphoreType.DMA((user_tiles,)),
            pltpu.SemaphoreType.DMA((item_tiles,)),
        ],
        compiler_params=pltpu.CompilerParams(vmem_limit_bytes=VMEM_GRANT),
        name="last_slot",
    )(users_then, blocks_then.reshape(slots, item_tiles, TILE, rank), ratings, *tables)
    return users_new.reshape(user_factors.shape), items_new.reshape(item_factors.shape)


def solution(mesh):
    both = ("wide", "narrow")
    in_specs = (
        P(both, None),
        P(both, None, None, None),
        P(both, None, None, None),
        P(both, None, None, None),
        P(both, None, None),
        P(both, None, None, None, None, None),
    )
    out_specs = (P(both, None), P(both, None, None, None))
    run = functools.partial(body, mesh.shape["wide"], mesh.shape["narrow"])
    return jax.shard_map(run, mesh=mesh, in_specs=in_specs, out_specs=out_specs, check_vma=False)
```
